512 devices in a mesh: tok: 128 (over z, y, core), head: 4 (over x).
Axes of the slice: x: 4, y: 8, z: 8, core: 2. Of those that a mesh axis runs over, the one named last changes fastest.
Arguments:
- query_rows: bfloat16 [24576, 1536], P('tok', 'head'), may hold values from -5 to 5
- key_rows: bfloat16 [24576, 1536], P('tok', 'head'), may hold values from -5 to 5
- value_rows: bfloat16 [24576, 1536], P('tok', 'head'), may hold values from -8 to 8
- neighbours: int32 [128, 27], replicated, may hold values from -1 to 127, as said below
- out_weight: bfloat16 [1536, 3072], P('head'), may hold values from -0.15625 to 0.15625
- out_grad: bfloat16 [24576, 3072], P(('tok', 'head')), may hold values from -6 to 6
Outputs:
- attended: bfloat16 [24576, 1536], P('tok', 'head')
- grad_queries: bfloat16 [24576, 1536], P('tok', 'head')
- grad_keys: bfloat16 [24576, 1536], P('tok', 'head')
- grad_values: bfloat16 [24576, 1536], P('tok', 'head')
The draws below stay inside these ranges and needn't reach their ends.
Inputs may be any that keep to these rules, and one draw needn't show every extreme that they name: `neighbours`: tile t lies at time tile t % 1 of device block b = t, and block b at tile row b // 8 and tile column b % 8 of a grid of 16 x 8 blocks. Entry (a + 1) * 9 + (b + 1) * 3 + (c + 1) of a tile's list, for a, b, c in -1, 0, 1, is either -1 or the tile displaced by a time tiles, b tile rows and c tile columns inside the grid; entry 13 is the tile itself; the listed tiles form a box around it.
All inputs are finite; a program needn't handle non-finite values.
Results may differ from the reference program's by a relative error of at most 0.02.
Values may be sent and summed in bfloat16 or wider, within the bound.
A program may use at most 64 MiB of HBM per device.

```python
import math
import jax
import jax.numpy as jnp
from jax import lax

D = 3072
HEADS = 12
HEAD_DIM = 128
TIME_TILES = 1
GRID_W = 8
SLOTS = 27
GRID_H = 16
TILE = 192
ROWS = 192
NT = 128
TOKENS = 24576


limit_value = 5.0


def draw_query_rows(key, part):
    key = jax.random.fold_in(key, 1)
    return jnp.clip(1.4 * jax.random.normal(key, (TOKENS, HEADS * HEAD_DIM), jnp.float32), -limit_value, limit_value).astype(jnp.bfloat16)


def draw_key_rows(key, part):
    key = jax.random.fold_in(key, 2)
    return jnp.clip(1.4 * jax.random.normal(key, (TOKENS, HEADS * HEAD_DIM), jnp.float32), -limit_value, limit_value).astype(jnp.bfloat16)


def inside_range(position, offset_step, length_limit, lower_flag, upper_flag):
    moved = position + offset_step
    return (moved >= 0) & (moved < length_limit) & ((offset_step != -1) | lower_flag) & ((offset_step != 1) | upper_flag)


def draw_neighbours(key, part):
    key = jax.random.fold_in(key, 3)
    extent_flags = jax.random.randint(key, (NT, 6), 0, 4) >= 1
    tile_ids = jnp.arange(NT)[:, None]
    block_ids = tile_ids // TIME_TILES
    time_index = tile_ids % TIME_TILES
    tile_row = block_ids // GRID_W
    tile_column = block_ids % GRID_W
    slot_ids = jnp.arange(SLOTS)[None, :]
    step_time = slot_ids // 9 - 1
    step_row = slot_ids // 3 % 3 - 1
    step_column = slot_ids % 3 - 1
    keep_entry = inside_range(time_index, step_time, TIME_TILES, extent_flags[:, 0:1], extent_flags[:, 1:2])
    keep_entry = keep_entry & inside_range(tile_row, step_row, GRID_H, extent_flags[:, 2:3], extent_flags[:, 3:4])
    keep_entry = keep_entry & inside_range(tile_column, step_column, GRID_W, extent_flags[:, 4:5], extent_flags[:, 5:6])
    target = ((tile_row + step_row) * GRID_W + tile_column + step_column) * TIME_TILES + time_index + step_time
    return jnp.where(keep_entry, target, -1).astype(jnp.int32)


def levels(stream_key, dims, cuts, low, high):
    level = 1.0
    for dim, blocks in cuts:
        draws = jax.random.uniform(jax.random.fold_in(jax.random.fold_in(stream_key, 6), dim), (blocks,), jnp.float32, low / len(cuts), high / len(cuts))
        level = level * jnp.repeat(jnp.exp(draws), dims[dim] // blocks).reshape((-1,) + (1,) * (len(dims) - 1 - dim))
    return level


def gaussian(key, shape, spread, bound, pieces=(), held_as=jnp.bfloat16):
    drawn = spread * jax.random.normal(key, shape, jnp.float32)
    if pieces:
        drawn = drawn * levels(key, shape, pieces, -0.22, 0.18)
    return jnp.clip(drawn, -bound, bound).astype(held_as)


def setup_inputs(seed: int = 0) -> dict:
    splits = jax.random.split(jax.random.key(seed), 7)
    query_rows = draw_query_rows(jax.random.fold_in(splits[6], 71), 0)
    key_rows = draw_key_rows(jax.random.fold_in(splits[6], 71), 0)
    value_rows = gaussian(splits[2], (TOKENS, HEADS * HEAD_DIM), 2.0, 8.0, ((0, 128), (1, 4)))
    neighbours = draw_neighbours(jax.random.fold_in(splits[6], 71), 0)
    out_weight = gaussian(splits[4], (HEADS * HEAD_DIM, D), (HEADS * HEAD_DIM) ** -0.5, 0.15625, ((0, 4),))
    out_grad = gaussian(splits[5], (TOKENS, D), 1.0, 6.0, ((0, 512),))
    return dict(query_rows=query_rows, key_rows=key_rows, value_rows=value_rows, neighbours=neighbours, out_weight=out_weight, out_grad=out_grad)


def reference(query_rows, key_rows, value_rows, neighbours, out_weight, out_grad):
    score_scale = 1.0 / math.sqrt(HEAD_DIM)
    block_total = NT // TIME_TILES
    block_shape = (block_total, ROWS, HEADS, HEAD_DIM)
    query_blocks = query_rows.reshape(block_shape)
    key_blocks = key_rows.reshape(block_shape)
    value_blocks = value_rows.reshape(block_shape)
    attended_grad = jnp.dot(out_grad, out_weight.T, preferred_element_type=jnp.float32).astype(jnp.bfloat16)
    grad_blocks = attended_grad.reshape(block_shape)
    slot_ids = jnp.arange(9, dtype=jnp.int32)
    row_step = slot_ids // 3 - 1
    column_step = slot_ids % 3 - 1
    time_ids = jnp.arange(TIME_TILES, dtype=jnp.int32)

    def visit_block(totals, block_id):
        grad_key_sum, grad_value_sum = totals
        block_row = block_id // GRID_W
        block_column = block_id % GRID_W
        near_row = block_row + row_step
        near_column = block_column + column_step
        valid = (near_row >= 0) & (near_row < GRID_H) & (near_column >= 0) & (near_column < GRID_W)
        near_block = jnp.where(valid, near_row * GRID_W + near_column, 0).astype(jnp.int32)
        key_tile_ids = jnp.where(valid[:, None], near_block[:, None] * TIME_TILES + time_ids[None, :], -2).astype(jnp.int32)
        own_lists = lax.dynamic_slice_in_dim(neighbours, (block_id * TIME_TILES).astype(jnp.int32), TIME_TILES, 0)
        allowed = jnp.any(own_lists[:, None, None, :] == key_tile_ids[None, :, :, None], axis=-1)
        allowed_rows = jnp.broadcast_to(allowed[:, None, :, :, None], (TIME_TILES, TILE, 9, TIME_TILES, TILE)).reshape(ROWS, 9 * ROWS)
        query_block = query_blocks[block_id].astype(jnp.float32)
        grad_block = grad_blocks[block_id].astype(jnp.float32)
        near_keys = key_blocks[near_block].reshape(9 * ROWS, HEADS, HEAD_DIM).astype(jnp.float32)
        near_values = value_blocks[near_block].reshape(9 * ROWS, HEADS, HEAD_DIM).astype(jnp.float32)
        scores = jnp.einsum('qhe,khe->hqk', query_block, near_keys) * score_scale
        scores = jnp.where(allowed_rows[None], scores, -jnp.inf)
        row_max = lax.optimization_barrier(jnp.max(scores, axis=2, keepdims=True))
        logsum = row_max + jnp.log(lax.optimization_barrier(jnp.sum(jnp.exp(scores - row_max), axis=2, keepdims=True)))
        weights = lax.optimization_barrier(jnp.exp(scores - logsum).astype(jnp.bfloat16)).astype(jnp.float32)
        attended = lax.optimization_barrier(jnp.einsum('hqk,khe->qhe', weights, near_values).astype(jnp.bfloat16))
        row_delta = lax.optimization_barrier(jnp.sum(grad_block * attended.astype(jnp.float32), axis=2))
        dprobs = jnp.einsum('qhe,khe->hqk', grad_block, near_values)
        dscores = weights * (dprobs - row_delta.T[:, :, None]) * score_scale
        dscores = lax.optimization_barrier(dscores.astype(jnp.bfloat16)).astype(jnp.float32)
        grad_query = jnp.einsum('hqk,khe->qhe', dscores, near_keys).astype(jnp.bfloat16)
        keep_weight = valid.astype(jnp.float32)[:, None, None, None]
        key_term = lax.optimization_barrier(jnp.einsum('hqk,qhe->khe', dscores, query_block).astype(jnp.bfloat16)).astype(jnp.float32)
        value_term = lax.optimization_barrier(jnp.einsum('hqk,qhe->khe', weights, grad_block).astype(jnp.bfloat16)).astype(jnp.float32)
        grad_key_sum = grad_key_sum.at[near_block].add(key_term.reshape(9, ROWS, HEADS, HEAD_DIM) * keep_weight)
        grad_value_sum = grad_value_sum.at[near_block].add(value_term.reshape(9, ROWS, HEADS, HEAD_DIM) * keep_weight)
        return ((grad_key_sum, grad_value_sum), (attended, grad_query))
    zeroes = jnp.zeros(block_shape, jnp.float32)
    (grad_key_sum, grad_value_sum), (attended, grad_query) = lax.scan(visit_block, (zeroes, zeroes), jnp.arange(block_total, dtype=jnp.int32))
    flat_shape = (TOKENS, HEADS * HEAD_DIM)
    return (attended.reshape(flat_shape), grad_query.reshape(flat_shape), grad_key_sum.reshape(flat_shape).astype(jnp.bfloat16), grad_value_sum.reshape(flat_shape).astype(jnp.bfloat16))
```

```python
import functools
import math

import jax
import jax.numpy as jnp
from jax import lax
from jax.experimental import pallas as pl
from jax.experimental.pallas import tpu as pltpu
from jax.sharding import PartitionSpec as P

MESH = pl.DeviceIdType.MESH
HEAD_DIM = 128
F1, F2, F3, F4, F5, F6A, F6B, F7 = range(8)
R1, R2, R3, R4, R5, R6A, R6B, R7 = range(8, 16)
STEPS = 16
F32 = jnp.float32
BF16 = jnp.bfloat16


def dot_nt(a, b):
    return lax.dot_general(a, b, (((1,), (1,)), ((), ())), preferred_element_type=F32)


def dot_nn(a, b):
    return lax.dot_general(a, b, (((1,), (0,)), ((), ())), preferred_element_type=F32)


def dot_tn(a, b):
    return lax.dot_general(a, b, (((0,), (0,)), ((), ())), preferred_element_type=F32)


def kernel(
    heads, rows, nz, ny, nx,
    q_hbm, k_hbm, v_hbm, nb_hbm, w_hbm, g_hbm,
    o_hbm, dq_hbm, dk_hbm, dv_hbm,
    nb, q, kv, w, g, grad, grad_t, scores, probs, stats, out_t, part, send, recv, outs,
    load_sem, store_sem, send_sem, recv_sem, x_send, x_recv,
):
    position = lax.axis_index("tok")
    x = lax.axis_index("head")
    core = lax.rem(position, 2)
    y = lax.rem(position // 2, ny)
    z = position // (2 * ny)
    y_half = y // (ny // 2)
    side = 2 * core - 1
    other = 1 - core
    dz = 1 - 2 * y_half

    def tok_at(z_, y_, core_):
        return (lax.rem(z_ + nz, nz) * ny + lax.rem(y_ + ny, ny)) * 2 + core_

    partner = (tok_at(z, y, other), x)
    outer = (tok_at(z, y + side, other), x)
    far = (tok_at(z, y + ny // 2 + side, other), x)
    z_next = (tok_at(z + dz, y, core), x)
    z_prev = (tok_at(z - dz, y, core), x)
    x_right = (position, lax.rem(x + 1, nx))
    x_left = (position, lax.rem(x + nx - 1, nx))
    peers = [partner, outer, far, z_next, z_prev, x_right, x_left]

    d_model = w.shape[1]
    half = d_model // 2
    scale = 1.0 / math.sqrt(HEAD_DIM)
    scale2 = scale * math.log2(math.e)

    def load(src, dst, index):
        return pltpu.make_async_copy(src, dst, load_sem.at[index])

    def columns(h):
        return pl.ds(h * HEAD_DIM, HEAD_DIM)

    own = pl.ds(0, rows)

    def tile(i):
        return pl.ds(i * rows, rows)

    x_rows = pl.multiple_of(x * (rows // nx), rows // nx)
    my_rows = pl.ds(x_rows, rows // nx)
    loads = {}
    for h in range(heads):
        loads["k", h] = load(k_hbm.at[:, columns(h)], kv.at[h, 0, 0, own], 3 * h)
        loads["v", h] = load(v_hbm.at[:, columns(h)], kv.at[h, 0, 1, own], 3 * h + 1)
        loads["q", h] = load(q_hbm.at[:, columns(h)], q.at[h], 3 * h + 2)
    loads["g"] = load(g_hbm, g.at[my_rows], 3 * heads)
    loads["nb"] = load(nb_hbm, nb, 3 * heads + 1)
    loads["w"] = load(w_hbm, w, 3 * heads + 2)
    for h in range(heads):
        loads["k", h].start()
        loads["v", h].start()
    loads["g"].start()
    for h in range(heads):
        loads["q", h].start()
    loads["nb"].start()
    loads["w"].start()

    barrier = pltpu.get_barrier_semaphore()
    for peer in peers:
        pl.semaphore_signal(barrier, inc=1, device_id=peer, device_id_type=MESH)
    pl.semaphore_wait(barrier, len(peers))

    def remote(h, step, src, dst, device):
        return pltpu.make_async_remote_copy(
            src_ref=src, dst_ref=dst, send_sem=send_sem.at[h, step], recv_sem=recv_sem.at[h, step],
            device_id=device, device_id_type=MESH,
        )

    def keys_of(h, group, index):
        return kv.at[h, group, :, tile(index)]

    copies = {}
    for h in range(heads):
        copies[h, F1] = remote(h, F1, keys_of(h, 0, 0), keys_of(h, 0, 1), partner)
        copies[h, F2] = remote(h, F2, keys_of(h, 0, 0), keys_of(h, 0, 2), outer)
        copies[h, F3] = remote(h, F3, keys_of(h, 0, 0), keys_of(h, 1, 0), far)
        copies[h, F4] = remote(h, F4, keys_of(h, 1, 0), keys_of(h, 1, 1), outer)
        copies[h, F5] = remote(h, F5, keys_of(h, 1, 1), keys_of(h, 1, 2), partner)
        copies[h, F6A] = remote(h, F6A, keys_of(h, 1, 0), keys_of(h, 2, 0), z_next)
        copies[h, F6B] = remote(h, F6B, keys_of(h, 1, 1), keys_of(h, 2, 1), z_next)
        copies[h, F7] = remote(h, F7, keys_of(h, 2, 1), keys_of(h, 2, 2), partner)
        back = {R1: partner, R2: outer, R3: far, R4: outer, R5: partner, R6A: z_prev, R6B: z_prev, R7: partner}
        for step, device in back.items():
            copies[h, step] = remote(h, step, send.at[h, step - R1], recv.at[h, step - R1], device)

    def start(h, *steps):
        for step in steps:
            copies[h, step].start()

    def arrive(h, *steps):
        for step in steps:
            copies[h, step].wait_recv()

    def x_copy(index, row_block, column_block, device):
        block = g.at[pl.ds(row_block, rows // nx), pl.ds(column_block * half, half)]
        return pltpu.make_async_remote_copy(
            src_ref=block, dst_ref=block, send_sem=x_send.at[index], recv_sem=x_recv.at[index],
            device_id=device, device_id_type=MESH,
        )

    left_rows = pl.multiple_of(lax.rem(x + nx - 1, nx) * (rows // nx), rows // nx)
    right_rows = pl.multiple_of(lax.rem(x + 1, nx) * (rows // nx), rows // nx)
    x_copies = [
        x_copy(0, x_rows, 0, x_right),
        x_copy(1, x_rows, 1, x_left),
        x_copy(2, x_rows, 1, x_right),
        x_copy(3, x_rows, 0, x_left),
        x_copy(4, left_rows, 0, x_right),
        x_copy(5, right_rows, 1, x_left),
    ]

    toward = 1 - 2 * y_half
    row_offset = (0, toward, -toward)

    def entries(group):
        base = 9 + (row_offset[group] + 1) * 3 + 1
        if group == 0:
            return (base, base - side, base + side)
        return (base + side, base, base - side)

    def relay1(h):
        arrive(h, F3)
        start(h, F4, F6A)

    def relay2(h):
        arrive(h, F4)
        start(h, F5, F6B)

    def relay3(h):
        arrive(h, F6B)
        start(h, F7)

    def x_relay():
        x_copies[0].wait_recv()
        x_copies[4].start()
        x_copies[1].wait_recv()
        x_copies[5].start()

    def forward(h, group):
        if group == 0:
            loads["q", h].wait()
            arrive(h, F1, F2)
        elif group == 1:
            arrive(h, F5)
        else:
            arrive(h, F6A, F7)
        query = q[h]
        top = jnp.full((1, rows), -1e30, F32)
        for i, entry in enumerate(entries(group)):
            bias = jnp.where(nb[position, entry] >= 0, 0.0, -jnp.inf).astype(F32)
            s = dot_nt(kv[h, group, 0, tile(i)], query) * scale2 + bias
            scores[tile(i)] = s
            top = jnp.maximum(top, jnp.max(s, axis=0, keepdims=True))
        total = jnp.zeros((1, rows), F32)
        attended = jnp.zeros((HEAD_DIM, rows), F32)
        for i in range(3):
            p = jnp.exp2(scores[tile(i)] - top)
            total = total + jnp.sum(p, axis=0, keepdims=True)
            p = p.astype(BF16)
            probs[h, group, tile(i)] = p
            attended = attended + dot_tn(kv[h, group, 1, tile(i)], p)
        stats[h, group, 0:1] = top
        stats[h, group, 1:2] = total
        out_t[h, group] = attended

    def project():
        loads["w"].wait()
        for index in range(2, 6):
            x_copies[index].wait_recv()
        whole = g[...]
        for h in range(heads):
            gt = dot_nt(w[pl.ds(h * HEAD_DIM, HEAD_DIM)], whole)
            grad_t[h] = gt.astype(BF16)
            grad[h] = gt.T.astype(BF16)

    def combine(h):
        tops = [stats[h, group, 0:1] for group in range(3)]
        top = jnp.maximum(jnp.maximum(tops[0], tops[1]), tops[2])
        factors = [jnp.exp2(t - top) for t in tops]
        total = sum(f * stats[h, group, 1:2] for group, f in enumerate(factors))
        attended = jnp.zeros((HEAD_DIM, rows), F32)
        for group in range(3):
            factor = factors[group] / total
            stats[h, group, 2:3] = factor
            attended = attended + out_t[h, group] * factor
        attended = attended.astype(BF16).astype(F32)
        stats[h, 0, 3:4] = jnp.sum(attended * grad_t[h].astype(F32), axis=0, keepdims=True)
        outs[0, h] = attended.T.astype(BF16)
        pltpu.make_async_copy(outs.at[0, h], o_hbm.at[:, columns(h)], store_sem.at[0, h]).start()

    def backward(h, group, emit):
        factor = stats[h, group, 2:3]
        delta = stats[h, 0, 3:4]
        query = q[h]
        grad_rows = grad[h]
        grad_cols = grad_t[h]
        query_t = jnp.zeros((HEAD_DIM, rows), F32)
        for i in range(3):
            weights = (probs[h, group, tile(i)].astype(F32) * factor).astype(BF16)
            dprobs = dot_nn(kv[h, group, 1, tile(i)], grad_cols)
            dscores = (weights.astype(F32) * ((dprobs - delta) * scale)).astype(BF16)
            query_t = query_t + dot_tn(kv[h, group, 0, tile(i)], dscores)
            emit(i, dot_nn(dscores, query), dot_nn(weights, grad_rows))
        if group == 2:
            out_t[h, 0] = query_t
        elif group == 1:
            out_t[h, 0] += query_t
        else:
            outs[1, h] = (out_t[h, 0] + query_t).T.astype(BF16)
            pltpu.make_async_copy(outs.at[1, h], dq_hbm.at[:, columns(h)], store_sem.at[1, h]).start()

    def put(h, step, dk, dv):
        send[h, step - R1, 0] = dk.astype(BF16)
        send[h, step - R1, 1] = dv.astype(BF16)
        start(h, step)

    def keep(h, slot, dk, dv):
        part[h, slot, 0] = dk
        part[h, slot, 1] = dv

    def emit_side(h):
        def emit(i, dk, dv):
            if i == 0:
                put(h, R6A, dk, dv)
            elif i == 1:
                keep(h, 0, dk, dv)
            else:
                put(h, R7, dk, dv)
        return emit

    def emit_far(h):
        def emit(i, dk, dv):
            if i == 0:
                keep(h, 1, dk, dv)
            elif i == 1:
                keep(h, 2, dk, dv)
            else:
                put(h, R5, dk, dv)
        return emit

    def emit_own(h):
        def emit(i, dk, dv):
            if i == 0:
                keep(h, 3, dk, dv)
            elif i == 1:
                put(h, R1, dk, dv)
            else:
                put(h, R2, dk, dv)
        return emit

    def gather_sum(h, slot, step, *steps):
        arrive(h, *steps)
        for i in range(2):
            total = part[h, slot, i]
            for other_step in steps:
                total = total + recv[h, other_step - R1, i].astype(F32)
            send[h, step - R1, i] = total.astype(BF16)
        start(h, step)

    def back2(h):
        backward(h, 2, emit_side(h))

    def back1(h):
        backward(h, 1, emit_far(h))

    def back0(h):
        backward(h, 0, emit_own(h))

    def sum_side(h):
        gather_sum(h, 0, R6B, R7)

    def sum_far(h):
        gather_sum(h, 2, R4, R5, R6B)

    def sum_outer(h):
        gather_sum(h, 1, R3, R6A, R4)

    def finish(h):
        arrive(h, R1, R2, R3)
        for i, out in enumerate((dk_hbm, dv_hbm)):
            total = part[h, 3, i]
            for step in (R1, R2, R3):
                total = total + recv[h, step - R1, i].astype(F32)
            outs[2 + i, h] = total.astype(BF16)
            pltpu.make_async_copy(outs.at[2 + i, h], out.at[:, columns(h)], store_sem.at[2 + i, h]).start()

    for h in range(heads):
        loads["k", h].wait()
        loads["v", h].wait()
        start(h, F3, F2, F1)
    loads["g"].wait()
    for index in range(4):
        x_copies[index].start()
    loads["nb"].wait()

    relay1(0)
    forward(0, 0)
    x_relay()
    relay2(0)
    relay1(1)
    forward(1, 0)
    relay2(1)
    forward(0, 1)
    relay1(2)
    relay3(0)
    forward(2, 0)
    relay2(2)
    forward(1, 1)
    relay3(1)
    forward(0, 2)
    project()
    combine(0)
    back2(0)
    relay3(2)
    forward(2, 1)
    forward(1, 2)
    sum_side(0)
    back1(0)
    combine(1)
    back2(1)
    sum_far(0)
    forward(2, 2)
    back0(0)
    sum_side(1)
    sum_outer(0)
    back1(1)
    combine(2)
    back2(2)
    sum_far(1)
    back0(1)
    sum_side(2)
    back1(2)
    sum_outer(1)
    finish(0)
    sum_far(2)
    back0(2)
    finish(1)
    sum_outer(2)
    finish(2)

    for h in range(heads):
        for step in range(STEPS):
            copies[h, step].wait_send()
        for i, out in enumerate((o_hbm, dq_hbm, dk_hbm, dv_hbm)):
            pltpu.make_async_copy(outs.at[i, h], out.at[:, columns(h)], store_sem.at[i, h]).wait()
    for copy in x_copies:
        copy.wait_send()


def local(nz, ny, nx, query_rows, key_rows, value_rows, neighbours, out_weight, out_grad):
    rows, width = query_rows.shape
    heads = width // HEAD_DIM
    d_model = out_weight.shape[1]
    any_spec = pl.BlockSpec(memory_space=pl.ANY)
    return pl.pallas_call(
        functools.partial(kernel, heads, rows, nz, ny, nx),
        out_shape=[jax.ShapeDtypeStruct((rows, width), BF16)] * 4,
        in_specs=[any_spec] * 6,
        out_specs=[any_spec] * 4,
        scratch_shapes=[
            pltpu.SMEM(neighbours.shape, jnp.int32),
            pltpu.VMEM((heads, rows, HEAD_DIM), BF16),
            pltpu.VMEM((heads, 3, 2, 3 * rows, HEAD_DIM), BF16),
            pltpu.VMEM((width, d_model), BF16),
            pltpu.VMEM((rows, d_model), BF16),
            pltpu.VMEM((heads, rows, HEAD_DIM), BF16),
            pltpu.VMEM((heads, HEAD_DIM, rows), BF16),
            pltpu.VMEM((3 * rows, rows), F32),
            pltpu.VMEM((heads, 3, 3 * rows, rows), BF16),
            pltpu.VMEM((heads, 3, 8, rows), F32),
            pltpu.VMEM((heads, 3, HEAD_DIM, rows), F32),
            pltpu.VMEM((heads, 4, 2, rows, HEAD_DIM), F32),
            pltpu.VMEM((heads, 8, 2, rows, HEAD_DIM), BF16),
            pltpu.VMEM((heads, 8, 2, rows, HEAD_DIM), BF16),
            pltpu.VMEM((4, heads, rows, HEAD_DIM), BF16),
            pltpu.SemaphoreType.DMA((3 * heads + 3,)),
            pltpu.SemaphoreType.DMA((4, heads)),
            pltpu.SemaphoreType.DMA((heads, STEPS)),
            pltpu.SemaphoreType.DMA((heads, STEPS)),
            pltpu.SemaphoreType.DMA((6,)),
            pltpu.SemaphoreType.DMA((6,)),
        ],
        compiler_params=pltpu.CompilerParams(
            collective_id=0, has_side_effects=True, vmem_limit_bytes=48 * 1024 * 1024
        ),
    )(query_rows, key_rows, value_rows, neighbours, out_weight, out_grad)


def solution(mesh):
    nx = mesh.shape["head"]
    ny = 8
    nz = mesh.shape["tok"] // (2 * ny)
    in_specs = (
        P("tok", "head"),
        P("tok", "head"),
        P("tok", "head"),
        P(),
        P("head", None),
        P(("tok", "head"), None),
    )
    out_specs = (P("tok", "head"), P("tok", "head"), P("tok", "head"), P("tok", "head"))
    return jax.shard_map(
        functools.partial(local, nz, ny, nx), mesh=mesh, in_specs=in_specs, out_specs=out_specs, check_vma=False
    )
```

```python
import functools
import math

import jax
import jax.numpy as jnp
from jax import lax
from jax.experimental import pallas as pl
from jax.experimental.pallas import tpu as pltpu
from jax.sharding import PartitionSpec as P

MESH = pl.DeviceIdType.MESH
HEAD_DIM = 128
F1, F2, F3, F4, F5, F6A, F6B, F7 = range(8)
R1, R2, R3, R4, R5, R6A, R6B, R7 = range(8, 16)
STEPS = 16
F32 = jnp.float32
BF16 = jnp.bfloat16


def dot_nt(a, b):
    return lax.dot_general(a, b, (((1,), (1,)), ((), ())), preferred_element_type=F32)


def dot_nn(a, b):
    return lax.dot_general(a, b, (((1,), (0,)), ((), ())), preferred_element_type=F32)


def dot_tn(a, b):
    return lax.dot_general(a, b, (((0,), (0,)), ((), ())), preferred_element_type=F32)


def kernel(
    heads, rows, nz, ny, nx,
    q_hbm, k_hbm, v_hbm, nb_hbm, w_hbm, g_hbm,
    packed,
    nb, q, kv, w, g, grad, grad_t, scores, probs, stats, out_t, part, send, recv, outs,
    load_sem, store_sem, send_sem, recv_sem, x_send, x_recv,
):
    position = lax.axis_index("tok")
    x = lax.axis_index("head")
    core = lax.rem(position, 2)
    y = lax.rem(position // 2, ny)
    z = position // (2 * ny)
    y_half = y // (ny // 2)
    side = 2 * core - 1
    other = 1 - core
    dz = 1 - 2 * y_half

    def tok_at(z_, y_, core_):
        return (lax.rem(z_ + nz, nz) * ny + lax.rem(y_ + ny, ny)) * 2 + core_

    partner = (tok_at(z, y, other), x)
    outer = (tok_at(z, y + side, other), x)
    far = (tok_at(z, y + ny // 2 + side, other), x)
    z_next = (tok_at(z + dz, y, core), x)
    z_prev = (tok_at(z - dz, y, core), x)
    x_right = (position, lax.rem(x + 1, nx))
    x_left = (position, lax.rem(x + nx - 1, nx))
    peers = [partner, outer, far, z_next, z_prev, x_right, x_left]

    d_model = w.shape[1]
    half = d_model // 2
    scale = 1.0 / math.sqrt(HEAD_DIM)
    scale2 = scale * math.log2(math.e)

    def load(src, dst, index):
        return pltpu.make_async_copy(src, dst, load_sem.at[index])

    def store(i, h):
        return pltpu.make_async_copy(outs.at[i, h], packed.at[i, h], store_sem.at[i, h])

    def columns(h):
        return pl.ds(h * HEAD_DIM, HEAD_DIM)

    own = pl.ds(0, rows)

    def tile(i):
        return pl.ds(i * rows, rows)

    x_rows = pl.multiple_of(x * (rows // nx), rows // nx)
    my_rows = pl.ds(x_rows, rows // nx)
    loads = {}
    for h in range(heads):
        loads["k", h] = load(k_hbm.at[:, columns(h)], kv.at[h, 0, 0, own], 3 * h)
        loads["v", h] = load(v_hbm.at[:, columns(h)], kv.at[h, 0, 1, own], 3 * h + 1)
        loads["q", h] = load(q_hbm.at[:, columns(h)], q.at[h], 3 * h + 2)
    loads["g"] = load(g_hbm, g.at[my_rows], 3 * heads)
    loads["nb"] = load(nb_hbm, nb, 3 * heads + 1)
    loads["w"] = load(w_hbm, w, 3 * heads + 2)
    for h in range(heads):
        loads["k", h].start()
        loads["v", h].start()
    loads["g"].start()
    for h in range(heads):
        loads["q", h].start()
    loads["nb"].start()
    loads["w"].start()

    barrier = pltpu.get_barrier_semaphore()
    for peer in peers:
        pl.semaphore_signal(barrier, inc=1, device_id=peer, device_id_type=MESH)
    pl.semaphore_wait(barrier, len(peers))

    def remote(h, step, src, dst, device):
        return pltpu.make_async_remote_copy(
            src_ref=src, dst_ref=dst, send_sem=send_sem.at[h, step], recv_sem=recv_sem.at[h, step],
            device_id=device, device_id_type=MESH,
        )

    def keys_of(h, group, index):
        return kv.at[h, group, :, tile(index)]

    copies = {}
    for h in range(heads):
        copies[h, F1] = remote(h, F1, keys_of(h, 0, 0), keys_of(h, 0, 1), partner)
        copies[h, F2] = remote(h, F2, keys_of(h, 0, 0), keys_of(h, 0, 2), outer)
        copies[h, F3] = remote(h, F3, keys_of(h, 0, 0), keys_of(h, 1, 0), far)
        copies[h, F4] = remote(h, F4, keys_of(h, 1, 0), keys_of(h, 1, 1), outer)
        copies[h, F5] = remote(h, F5, keys_of(h, 1, 1), keys_of(h, 1, 2), partner)
        copies[h, F6A] = remote(h, F6A, keys_of(h, 1, 0), keys_of(h, 2, 0), z_next)
        copies[h, F6B] = remote(h, F6B, keys_of(h, 1, 1), keys_of(h, 2, 1), z_next)
        copies[h, F7] = remote(h, F7, keys_of(h, 2, 1), keys_of(h, 2, 2), partner)
        back = {R1: partner, R2: outer, R3: far, R4: outer, R5: partner, R6A: z_prev, R6B: z_prev, R7: partner}
        for step, device in back.items():
            copies[h, step] = remote(h, step, send.at[h, step - R1], recv.at[h, step - R1], device)

    def start(h, *steps):
        for step in steps:
            copies[h, step].start()

    def arrive(h, *steps):
        for step in steps:
            copies[h, step].wait_recv()

    def x_copy(index, row_block, column_block, device):
        block = g.at[pl.ds(row_block, rows // nx), pl.ds(column_block * half, half)]
        return pltpu.make_async_remote_copy(
            src_ref=block, dst_ref=block, send_sem=x_send.at[index], recv_sem=x_recv.at[index],
            device_id=device, device_id_type=MESH,
        )

    left_rows = pl.multiple_of(lax.rem(x + nx - 1, nx) * (rows // nx), rows // nx)
    right_rows = pl.multiple_of(lax.rem(x + 1, nx) * (rows // nx), rows // nx)
    x_copies = [
        x_copy(0, x_rows, 0, x_right),
        x_copy(1, x_rows, 1, x_left),
        x_copy(2, x_rows, 1, x_right),
        x_copy(3, x_rows, 0, x_left),
        x_copy(4, left_rows, 0, x_right),
        x_copy(5, right_rows, 1, x_left),
    ]

    toward = 1 - 2 * y_half
    row_offset = (0, toward, -toward)

    def entries(group):
        base = 9 + (row_offset[group] + 1) * 3 + 1
        if group == 0:
            return (base, base - side, base + side)
        return (base + side, base, base - side)

    def relay1(h):
        arrive(h, F3)
        start(h, F4, F6A, F2)

    def relay2(h):
        arrive(h, F4)
        start(h, F5, F6B)

    def relay3(h):
        arrive(h, F6B)
        start(h, F7)

    def x_relay():
        x_copies[0].wait_recv()
        x_copies[4].start()
        x_copies[1].wait_recv()
        x_copies[5].start()

    def forward(h, group):
        if group == 0:
            arrive(h, F1, F2)
        elif group == 1:
            arrive(h, F5)
        else:
            arrive(h, F6A, F7)
        query = q[h]
        top = jnp.full((1, rows), -1e30, F32)
        for i, entry in enumerate(entries(group)):
            bias = jnp.where(nb[entry, position] >= 0, 0.0, -jnp.inf).astype(F32)
            s = dot_nt(kv[h, group, 0, tile(i)], query) * scale2 + bias
            scores[tile(i)] = s
            top = jnp.maximum(top, jnp.max(s, axis=0, keepdims=True))
        total = jnp.zeros((1, rows), F32)
        attended = jnp.zeros((HEAD_DIM, rows), F32)
        for i in range(3):
            p = jnp.exp2(scores[tile(i)] - top)
            total = total + jnp.sum(p, axis=0, keepdims=True)
            p = p.astype(BF16)
            probs[h, group, tile(i)] = p
            attended = attended + dot_tn(kv[h, group, 1, tile(i)], p)
        stats[h, group, 0:1] = top
        stats[h, group, 1:2] = total
        out_t[h, group] = attended

    def project():
        loads["w"].wait()
        for index in range(2, 6):
            x_copies[index].wait_recv()
        whole = g[...]
        for h in range(heads):
            gt = dot_nt(w[pl.ds(h * HEAD_DIM, HEAD_DIM)], whole)
            grad_t[h] = gt.astype(BF16)
            grad[h] = gt.T.astype(BF16)

    def combine(h):
        tops = [stats[h, group, 0:1] for group in range(3)]
        top = jnp.maximum(jnp.maximum(tops[0], tops[1]), tops[2])
        factors = [jnp.exp2(t - top) for t in tops]
        total = sum(f * stats[h, group, 1:2] for group, f in enumerate(factors))
        attended = jnp.zeros((HEAD_DIM, rows), F32)
        for group in range(3):
            factor = factors[group] / total
            stats[h, group, 2:3] = factor
            attended = attended + out_t[h, group] * factor
        attended = attended.astype(BF16).astype(F32)
        stats[h, 0, 3:4] = jnp.sum(attended * grad_t[h].astype(F32), axis=0, keepdims=True)
        outs[0, h] = attended.T.astype(BF16)
        store(0, h).start()

    def backward(h, group, emit):
        factor = stats[h, group, 2:3]
        delta = stats[h, 0, 3:4]
        query = q[h]
        grad_rows = grad[h]
        grad_cols = grad_t[h]
        query_t = jnp.zeros((HEAD_DIM, rows), F32)
        for i in range(3):
            weights = (probs[h, group, tile(i)].astype(F32) * factor).astype(BF16)
            dprobs = dot_nn(kv[h, group, 1, tile(i)], grad_cols)
            dscores = (weights.astype(F32) * ((dprobs - delta) * scale)).astype(BF16)
            query_t = query_t + dot_tn(kv[h, group, 0, tile(i)], dscores)
            emit(i, dot_nn(dscores, query), dot_nn(weights, grad_rows))
        if group == 2:
            out_t[h, 0] = query_t
        elif group == 1:
            out_t[h, 0] += query_t
        else:
            outs[1, h] = (out_t[h, 0] + query_t).T.astype(BF16)
            store(1, h).start()

    def put(h, step, dk, dv):
        send[h, step - R1, 0] = dk.astype(BF16)
        send[h, step - R1, 1] = dv.astype(BF16)
        start(h, step)

    def keep(h, slot, dk, dv):
        part[h, slot, 0] = dk
        part[h, slot, 1] = dv

    def emit_side(h):
        def emit(i, dk, dv):
            if i == 0:
                put(h, R6A, dk, dv)
            elif i == 1:
                keep(h, 0, dk, dv)
            else:
                put(h, R7, dk, dv)
        return emit

    def emit_far(h):
        def emit(i, dk, dv):
            if i == 0:
                keep(h, 1, dk, dv)
            elif i == 1:
                keep(h, 2, dk, dv)
            else:
                put(h, R5, dk, dv)
        return emit

    def emit_own(h):
        def emit(i, dk, dv):
            if i == 0:
                keep(h, 3, dk, dv)
            elif i == 1:
                put(h, R1, dk, dv)
            else:
                put(h, R2, dk, dv)
        return emit

    def gather_sum(h, slot, step, *steps):
        arrive(h, *steps)
        for i in range(2):
            total = part[h, slot, i]
            for other_step in steps:
                total = total + recv[h, other_step - R1, i].astype(F32)
            send[h, step - R1, i] = total.astype(BF16)
        start(h, step)

    def back2(h):
        backward(h, 2, emit_side(h))

    def back1(h):
        backward(h, 1, emit_far(h))

    def back0(h):
        backward(h, 0, emit_own(h))

    def sum_side(h):
        gather_sum(h, 0, R6B, R7)

    def sum_far(h):
        gather_sum(h, 2, R4, R5, R6B)

    def sum_outer(h):
        gather_sum(h, 1, R3, R6A, R4)

    def finish(h):
        arrive(h, R1, R2, R3)
        for i in range(2):
            total = part[h, 3, i]
            for step in (R1, R2, R3):
                total = total + recv[h, step - R1, i].astype(F32)
            outs[2 + i, h] = total.astype(BF16)
            store(2 + i, h).start()

    for h in range(heads):
        loads["k", h].wait()
        loads["v", h].wait()
        start(h, F3, F1)
    loads["g"].wait()
    for index in range(4):
        x_copies[index].start()
    loads["nb"].wait()
    for h in range(heads):
        loads["q", h].wait()

    relay1(0)
    x_relay()
    relay2(0)
    forward(0, 1)
    relay1(1)
    forward(0, 0)
    relay3(0)
    project()
    forward(0, 2)
    relay2(1)
    combine(0)
    back2(0)
    forward(1, 1)
    sum_side(0)
    relay1(2)
    back1(0)
    relay3(1)
    forward(1, 0)
    back0(0)
    relay2(2)
    forward(1, 2)
    combine(1)
    back2(1)
    forward(2, 1)
    sum_side(1)
    relay3(2)
    back1(1)
    sum_far(0)
    forward(2, 0)
    forward(2, 2)
    combine(2)
    back2(2)
    back0(1)
    sum_side(2)
    sum_outer(0)
    back1(2)
    sum_far(1)
    back0(2)
    sum_outer(1)
    sum_far(2)
    finish(0)
    sum_outer(2)
    finish(1)
    finish(2)

    for h in range(heads):
        for step in range(STEPS):
            copies[h, step].wait_send()
        for i in range(4):
            store(i, h).wait()
    for copy in x_copies:
        copy.wait_send()


def unpack(heads, packed, *refs):
    results, scratch, in_sem, out_sem = refs[:4], refs[4], refs[5], refs[6]
    loads = []
    for i in range(4):
        for h in range(heads):
            block = scratch.at[i, :, pl.ds(h * HEAD_DIM, HEAD_DIM)]
            loads.append(pltpu.make_async_copy(packed.at[i, h], block, in_sem.at[i, h]))
    for copy in loads:
        copy.start()
    stores = [pltpu.make_async_copy(scratch.at[i], result, out_sem.at[i]) for i, result in enumerate(results)]
    for i in range(4):
        for h in range(heads):
            loads[i * heads + h].wait()
        stores[i].start()
    for copy in stores:
        copy.wait()


def local(nz, ny, nx, query_rows, key_rows, value_rows, neighbours, out_weight, out_grad):
    rows, width = query_rows.shape
    heads = width // HEAD_DIM
    d_model = out_weight.shape[1]
    hbm = pl.BlockSpec(memory_space=pltpu.HBM)
    packed = pl.pallas_call(
        functools.partial(kernel, heads, rows, nz, ny, nx),
        out_shape=jax.ShapeDtypeStruct((4, heads, rows, HEAD_DIM), BF16),
        in_specs=[hbm] * 6,
        out_specs=hbm,
        scratch_shapes=[
            pltpu.SMEM(neighbours.shape[::-1], jnp.int32),
            pltpu.VMEM((heads, rows, HEAD_DIM), BF16),
            pltpu.VMEM((heads, 3, 2, 3 * rows, HEAD_DIM), BF16),
            pltpu.VMEM((width, d_model), BF16),
            pltpu.VMEM((rows, d_model), BF16),
            pltpu.VMEM((heads, rows, HEAD_DIM), BF16),
            pltpu.VMEM((heads, HEAD_DIM, rows), BF16),
            pltpu.VMEM((3 * rows, rows), F32),
            pltpu.VMEM((heads, 3, 3 * rows, rows), BF16),
            pltpu.VMEM((heads, 3, 8, rows), F32),
            pltpu.VMEM((heads, 3, HEAD_DIM, rows), F32),
            pltpu.VMEM((heads, 4, 2, rows, HEAD_DIM), F32),
            pltpu.VMEM((heads, 8, 2, rows, HEAD_DIM), BF16),
            pltpu.VMEM((heads, 8, 2, rows, HEAD_DIM), BF16),
            pltpu.VMEM((4, heads, rows, HEAD_DIM), BF16),
            pltpu.SemaphoreType.DMA((3 * heads + 3,)),
            pltpu.SemaphoreType.DMA((4, heads)),
            pltpu.SemaphoreType.DMA((heads, STEPS)),
            pltpu.SemaphoreType.DMA((heads, STEPS)),
            pltpu.SemaphoreType.DMA((6,)),
            pltpu.SemaphoreType.DMA((6,)),
        ],
        compiler_params=pltpu.CompilerParams(
            collective_id=0, has_side_effects=True, vmem_limit_bytes=63 * 1024 * 1024
        ),
    )(query_rows, key_rows, value_rows, neighbours.T, out_weight, out_grad)
    return pl.pallas_call(
        functools.partial(unpack, heads),
        out_shape=[jax.ShapeDtypeStruct((rows, width), BF16)] * 4,
        in_specs=[hbm],
        out_specs=[hbm] * 4,
        scratch_shapes=[
            pltpu.VMEM((4, rows, width), BF16),
            pltpu.SemaphoreType.DMA((4, heads)),
            pltpu.SemaphoreType.DMA((4,)),
        ],
    )(packed)


def solution(mesh):
    nx = mesh.shape["head"]
    ny = 8
    nz = mesh.shape["tok"] // (2 * ny)
    in_specs = (
        P("tok", "head"),
        P("tok", "head"),
        P("tok", "head"),
        P(),
        P("head", None),
        P(("tok", "head"), None),
    )
    out_specs = (P("tok", "head"), P("tok", "head"), P("tok", "head"), P("tok", "head"))
    return jax.shard_map(
        functools.partial(local, nz, ny, nx), mesh=mesh, in_specs=in_specs, out_specs=out_specs, check_vma=False
    )
```

```python
import functools
import math

import jax
import jax.numpy as jnp
from jax import lax
from jax.experimental import pallas as pl
from jax.experimental.pallas import tpu as pltpu
from jax.sharding import PartitionSpec as P

MESH = pl.DeviceIdType.MESH
HEAD_DIM = 128
F1, F2, F3, F4, F5, F6A, F6B, F7 = range(8)
R1, R2, R3, R4, R5, R6A, R6B, R7 = range(8, 16)
STEPS = 16
SPLIT = (R3, R4, R6B, R7)
F32 = jnp.float32
BF16 = jnp.bfloat16


def dot_nt(a, b):
    return lax.dot_general(a, b, (((1,), (1,)), ((), ())), preferred_element_type=F32)


def dot_nn(a, b):
    return lax.dot_general(a, b, (((1,), (0,)), ((), ())), preferred_element_type=F32)


def dot_tn(a, b):
    return lax.dot_general(a, b, (((0,), (0,)), ((), ())), preferred_element_type=F32)


def kernel(
    heads, rows, nz, ny, nx,
    q_hbm, k_hbm, v_hbm, nb_hbm, w_hbm, g_hbm,
    packed,
    nb, q, kv, w, g, grad, grad_t, scores, probs, stats, out_t, part, send, recv, outs,
    load_sem, store_sem, send_sem, recv_sem, x_send, x_recv,
):
    position = lax.axis_index("tok")
    x = lax.axis_index("head")
    core = lax.rem(position, 2)
    y = lax.rem(position // 2, ny)
    z = position // (2 * ny)
    y_half = y // (ny // 2)
    side = 2 * core - 1
    other = 1 - core
    dz = 1 - 2 * y_half

    def tok_at(z_, y_, core_):
        return (lax.rem(z_ + nz, nz) * ny + lax.rem(y_ + ny, ny)) * 2 + core_

    partner = (tok_at(z, y, other), x)
    outer = (tok_at(z, y + side, other), x)
    far = (tok_at(z, y + ny // 2 + side, other), x)
    z_next = (tok_at(z + dz, y, core), x)
    z_prev = (tok_at(z - dz, y, core), x)
    x_right = (position, lax.rem(x + 1, nx))
    x_left = (position, lax.rem(x + nx - 1, nx))
    peers = [partner, outer, far, z_next, z_prev, x_right, x_left]

    d_model = w.shape[1]
    half = d_model // 2
    scale = 1.0 / math.sqrt(HEAD_DIM)
    scale2 = scale * math.log2(math.e)

    def load(src, dst, index):
        return pltpu.make_async_copy(src, dst, load_sem.at[index])

    def store(i, h):
        return pltpu.make_async_copy(outs.at[i, h], packed.at[i, h], store_sem.at[i, h])

    def columns(h):
        return pl.ds(h * HEAD_DIM, HEAD_DIM)

    own = pl.ds(0, rows)

    def tile(i):
        return pl.ds(i * rows, rows)

    x_rows = pl.multiple_of(x * (rows // nx), rows // nx)
    my_rows = pl.ds(x_rows, rows // nx)
    loads = {}
    for h in range(heads):
        loads["k", h] = load(k_hbm.at[:, columns(h)], kv.at[h, 0, 0, own], 3 * h)
        loads["v", h] = load(v_hbm.at[:, columns(h)], kv.at[h, 0, 1, own], 3 * h + 1)
        loads["q", h] = load(q_hbm.at[:, columns(h)], q.at[h], 3 * h + 2)
    loads["g"] = load(g_hbm, g.at[my_rows], 3 * heads)
    loads["nb"] = load(nb_hbm, nb, 3 * heads + 1)
    loads["w"] = load(w_hbm, w, 3 * heads + 2)
    for h in range(heads):
        loads["k", h].start()
        loads["v", h].start()
    loads["g"].start()
    for h in range(heads):
        loads["q", h].start()
    loads["nb"].start()
    loads["w"].start()

    barrier = pltpu.get_barrier_semaphore()
    for peer in peers:
        pl.semaphore_signal(barrier, inc=1, device_id=peer, device_id_type=MESH)
    pl.semaphore_wait(barrier, len(peers))

    def remote(h, step, src, dst, device, half=0):
        return pltpu.make_async_remote_copy(
            src_ref=src, dst_ref=dst, send_sem=send_sem.at[h, step, half], recv_sem=recv_sem.at[h, step, half],
            device_id=device, device_id_type=MESH,
        )

    def keys_of(h, group, index):
        return kv.at[h, group, :, tile(index)]

    copies = {}
    for h in range(heads):
        copies[h, F1] = remote(h, F1, keys_of(h, 0, 0), keys_of(h, 0, 1), partner)
        copies[h, F2] = remote(h, F2, keys_of(h, 0, 0), keys_of(h, 0, 2), outer)
        copies[h, F3] = remote(h, F3, keys_of(h, 0, 0), keys_of(h, 1, 0), far)
        copies[h, F4] = remote(h, F4, keys_of(h, 1, 0), keys_of(h, 1, 1), outer)
        copies[h, F5] = remote(h, F5, keys_of(h, 1, 1), keys_of(h, 1, 2), partner)
        copies[h, F6A] = remote(h, F6A, keys_of(h, 1, 0), keys_of(h, 2, 0), z_next)
        copies[h, F6B] = remote(h, F6B, keys_of(h, 1, 1), keys_of(h, 2, 1), z_next)
        copies[h, F7] = remote(h, F7, keys_of(h, 2, 1), keys_of(h, 2, 2), partner)
        back = {R1: partner, R2: outer, R3: far, R4: outer, R5: partner, R6A: z_prev, R6B: z_prev, R7: partner}
        for step, device in back.items():
            here, there = send.at[h, step - R1], recv.at[h, step - R1]
            if step in SPLIT:
                for i in range(2):
                    copies[h, step, i] = remote(h, step, here.at[i], there.at[i], device, i)
            else:
                copies[h, step] = remote(h, step, here, there, device)

    def start(h, *steps):
        for step in steps:
            copies[h, step].start()

    def arrive(h, *steps):
        for step in steps:
            copies[h, step].wait_recv()

    def x_copy(index, row_block, column_block, device):
        block = g.at[pl.ds(row_block, rows // nx), pl.ds(column_block * half, half)]
        return pltpu.make_async_remote_copy(
            src_ref=block, dst_ref=block, send_sem=x_send.at[index], recv_sem=x_recv.at[index],
            device_id=device, device_id_type=MESH,
        )

    left_rows = pl.multiple_of(lax.rem(x + nx - 1, nx) * (rows // nx), rows // nx)
    right_rows = pl.multiple_of(lax.rem(x + 1, nx) * (rows // nx), rows // nx)
    x_copies = [
        x_copy(0, x_rows, 0, x_right),
        x_copy(1, x_rows, 1, x_left),
        x_copy(2, x_rows, 1, x_right),
        x_copy(3, x_rows, 0, x_left),
        x_copy(4, left_rows, 0, x_right),
        x_copy(5, right_rows, 1, x_left),
    ]

    toward = 1 - 2 * y_half
    row_offset = (0, toward, -toward)

    def entries(group):
        base = 9 + (row_offset[group] + 1) * 3 + 1
        if group == 0:
            return (base, base - side, base + side)
        return (base + side, base, base - side)

    def relay1(h):
        arrive(h, F3)
        start(h, F4, F6A, F2)

    def relay2(h):
        arrive(h, F4)
        start(h, F5, F6B)

    def relay3(h):
        arrive(h, F6B)
        start(h, F7)

    def x_relay():
        x_copies[0].wait_recv()
        x_copies[4].start()
        x_copies[1].wait_recv()
        x_copies[5].start()

    def forward(h, group):
        if group == 0:
            arrive(h, F1, F2)
        elif group == 1:
            arrive(h, F5)
        else:
            arrive(h, F6A, F7)
        query = q[h]
        top = jnp.full((1, rows), -1e30, F32)
        for i, entry in enumerate(entries(group)):
            bias = jnp.where(nb[entry, position] >= 0, 0.0, -jnp.inf).astype(F32)
            s = dot_nt(kv[h, group, 0, tile(i)], query) * scale2 + bias
            scores[tile(i)] = s
            top = jnp.maximum(top, jnp.max(s, axis=0, keepdims=True))
        total = jnp.zeros((1, rows), F32)
        attended = jnp.zeros((HEAD_DIM, rows), F32)
        for i in range(3):
            p = jnp.exp2(scores[tile(i)] - top)
            total = total + jnp.sum(p, axis=0, keepdims=True)
            p = p.astype(BF16)
            probs[h, group, tile(i)] = p
            attended = attended + dot_tn(kv[h, group, 1, tile(i)], p)
        stats[h, group, 0:1] = top
        stats[h, group, 1:2] = total
        out_t[h, group] = attended

    def project():
        loads["w"].wait()
        for index in range(2, 6):
            x_copies[index].wait_recv()
        whole = g[...]
        for h in range(heads):
            gt = dot_nt(w[pl.ds(h * HEAD_DIM, HEAD_DIM)], whole)
            grad_t[h] = gt.astype(BF16)
            grad[h] = gt.T.astype(BF16)

    def combine(h):
        tops = [stats[h, group, 0:1] for group in range(3)]
        top = jnp.maximum(jnp.maximum(tops[0], tops[1]), tops[2])
        factors = [jnp.exp2(t - top) for t in tops]
        total = sum(f * stats[h, group, 1:2] for group, f in enumerate(factors))
        attended = jnp.zeros((HEAD_DIM, rows), F32)
        for group in range(3):
            factor = factors[group] / total
            stats[h, group, 2:3] = factor
            attended = attended + out_t[h, group] * factor
        attended = attended.astype(BF16).astype(F32)
        stats[h, 0, 3:4] = jnp.sum(attended * grad_t[h].astype(F32), axis=0, keepdims=True)
        outs[0, h] = attended.T.astype(BF16)
        store(0, h).start()

    def backward(h, group, emit):
        factor = stats[h, group, 2:3]
        delta = stats[h, 0, 3:4]
        query = q[h]
        grad_rows = grad[h]
        grad_cols = grad_t[h]
        query_t = jnp.zeros((HEAD_DIM, rows), F32)
        for i in range(3):
            weights = (probs[h, group, tile(i)].astype(F32) * factor).astype(BF16)
            dprobs = dot_nn(kv[h, group, 1, tile(i)], grad_cols)
            dscores = (weights.astype(F32) * ((dprobs - delta) * scale)).astype(BF16)
            query_t = query_t + dot_tn(kv[h, group, 0, tile(i)], dscores)
            emit(i, dot_nn(dscores, query), dot_nn(weights, grad_rows))
        if group == 2:
            out_t[h, 0] = query_t
        elif group == 1:
            out_t[h, 0] += query_t
        else:
            outs[1, h] = (out_t[h, 0] + query_t).T.astype(BF16)
            store(1, h).start()

    def put(h, step, dk, dv):
        for i, term in enumerate((dk, dv)):
            send[h, step - R1, i] = term.astype(BF16)
            if step in SPLIT:
                copies[h, step, i].start()
        if step not in SPLIT:
            start(h, step)

    def keep(h, slot, dk, dv):
        part[h, slot, 0] = dk
        part[h, slot, 1] = dv

    def emit_side(h):
        def emit(i, dk, dv):
            if i == 0:
                put(h, R6A, dk, dv)
            elif i == 1:
                keep(h, 0, dk, dv)
            else:
                put(h, R7, dk, dv)
        return emit

    def emit_far(h):
        def emit(i, dk, dv):
            if i == 0:
                keep(h, 1, dk, dv)
            elif i == 1:
                keep(h, 2, dk, dv)
            else:
                put(h, R5, dk, dv)
        return emit

    def emit_own(h):
        def emit(i, dk, dv):
            if i == 0:
                keep(h, 3, dk, dv)
            elif i == 1:
                put(h, R1, dk, dv)
            else:
                put(h, R2, dk, dv)
        return emit

    def gather_sum(h, slot, step, *steps):
        for i in range(2):
            for other_step in steps:
                if other_step in SPLIT:
                    copies[h, other_step, i].wait_recv()
                elif i == 0:
                    arrive(h, other_step)
            total = part[h, slot, i]
            for other_step in steps:
                total = total + recv[h, other_step - R1, i].astype(F32)
            send[h, step - R1, i] = total.astype(BF16)
            copies[h, step, i].start()

    def back2(h):
        backward(h, 2, emit_side(h))

    def back1(h):
        backward(h, 1, emit_far(h))

    def back0(h):
        backward(h, 0, emit_own(h))

    def sum_side(h):
        gather_sum(h, 0, R6B, R7)

    def sum_far(h):
        gather_sum(h, 2, R4, R5, R6B)

    def sum_outer(h):
        gather_sum(h, 1, R3, R6A, R4)

    def finish(h):
        arrive(h, R1, R2)
        for i in range(2):
            copies[h, R3, i].wait_recv()
            total = part[h, 3, i]
            for step in (R1, R2, R3):
                total = total + recv[h, step - R1, i].astype(F32)
            outs[2 + i, h] = total.astype(BF16)
            store(2 + i, h).start()

    for h in range(heads):
        loads["k", h].wait()
        loads["v", h].wait()
        start(h, F3, F1)
    loads["g"].wait()
    for index in range(4):
        x_copies[index].start()
    loads["nb"].wait()
    for h in range(heads):
        loads["q", h].wait()

    relay1(0)
    x_relay()
    relay2(0)
    forward(0, 1)
    relay1(1)
    forward(0, 0)
    relay3(0)
    project()
    forward(0, 2)
    relay2(1)
    combine(0)
    back2(0)
    forward(1, 1)
    sum_side(0)
    relay1(2)
    back1(0)
    relay3(1)
    forward(1, 0)
    back0(0)
    relay2(2)
    forward(1, 2)
    combine(1)
    back2(1)
    forward(2, 1)
    sum_side(1)
    relay3(2)
    back1(1)
    sum_far(0)
    forward(2, 0)
    forward(2, 2)
    combine(2)
    back2(2)
    back0(1)
    sum_side(2)
    sum_outer(0)
    back1(2)
    sum_far(1)
    back0(2)
    sum_outer(1)
    sum_far(2)
    finish(0)
    sum_outer(2)
    finish(1)
    finish(2)

    for h in range(heads):
        for step in range(STEPS):
            for key in ([(h, step, 0), (h, step, 1)] if step in SPLIT else [(h, step)]):
                copies[key].wait_send()
        for i in range(4):
            store(i, h).wait()
    for copy in x_copies:
        copy.wait_send()


def unpack(heads, packed, *refs):
    results, scratch, in_sem, out_sem = refs[:4], refs[4], refs[5], refs[6]
    loads = []
    for i in range(4):
        for h in range(heads):
            block = scratch.at[i, :, pl.ds(h * HEAD_DIM, HEAD_DIM)]
            loads.append(pltpu.make_async_copy(packed.at[i, h], block, in_sem.at[i, h]))
    for copy in loads:
        copy.start()
    stores = [pltpu.make_async_copy(scratch.at[i], result, out_sem.at[i]) for i, result in enumerate(results)]
    for i in range(4):
        for h in range(heads):
            loads[i * heads + h].wait()
        stores[i].start()
    for copy in stores:
        copy.wait()


def local(nz, ny, nx, query_rows, key_rows, value_rows, neighbours, out_weight, out_grad):
    rows, width = query_rows.shape
    heads = width // HEAD_DIM
    d_model = out_weight.shape[1]
    hbm = pl.BlockSpec(memory_space=pltpu.HBM)
    packed = pl.pallas_call(
        functools.partial(kernel, heads, rows, nz, ny, nx),
        out_shape=jax.ShapeDtypeStruct((4, heads, rows, HEAD_DIM), BF16),
        in_specs=[hbm] * 6,
        out_specs=hbm,
        scratch_shapes=[
            pltpu.SMEM(neighbours.shape[::-1], jnp.int32),
            pltpu.VMEM((heads, rows, HEAD_DIM), BF16),
            pltpu.VMEM((heads, 3, 2, 3 * rows, HEAD_DIM), BF16),
            pltpu.VMEM((width, d_model), BF16),
            pltpu.VMEM((rows, d_model), BF16),
            pltpu.VMEM((heads, rows, HEAD_DIM), BF16),
            pltpu.VMEM((heads, HEAD_DIM, rows), BF16),
            pltpu.VMEM((3 * rows, rows), F32),
            pltpu.VMEM((heads, 3, 3 * rows, rows), BF16),
            pltpu.VMEM((heads, 3, 8, rows), F32),
            pltpu.VMEM((heads, 3, HEAD_DIM, rows), F32),
            pltpu.VMEM((heads, 4, 2, rows, HEAD_DIM), F32),
            pltpu.VMEM((heads, 8, 2, rows, HEAD_DIM), BF16),
            pltpu.VMEM((heads, 8, 2, rows, HEAD_DIM), BF16),
            pltpu.VMEM((4, heads, rows, HEAD_DIM), BF16),
            pltpu.SemaphoreType.DMA((3 * heads + 3,)),
            pltpu.SemaphoreType.DMA((4, heads)),
            pltpu.SemaphoreType.DMA((heads, STEPS, 2)),
            pltpu.SemaphoreType.DMA((heads, STEPS, 2)),
            pltpu.SemaphoreType.DMA((6,)),
            pltpu.SemaphoreType.DMA((6,)),
        ],
        compiler_params=pltpu.CompilerParams(
            collective_id=0, has_side_effects=True, vmem_limit_bytes=63 * 1024 * 1024
        ),
    )(query_rows, key_rows, value_rows, neighbours.T, out_weight, out_grad)
    return pl.pallas_call(
        functools.partial(unpack, heads),
        out_shape=[jax.ShapeDtypeStruct((rows, width), BF16)] * 4,
        in_specs=[hbm],
        out_specs=[hbm] * 4,
        scratch_shapes=[
            pltpu.VMEM((4, rows, width), BF16),
            pltpu.SemaphoreType.DMA((4, heads)),
            pltpu.SemaphoreType.DMA((4,)),
        ],
    )(packed)


def solution(mesh):
    nx = mesh.shape["head"]
    ny = 8
    nz = mesh.shape["tok"] // (2 * ny)
    in_specs = (
        P("tok", "head"),
        P("tok", "head"),
        P("tok", "head"),
        P(),
        P("head", None),
        P(("tok", "head"), None),
    )
    out_specs = (P("tok", "head"), P("tok", "head"), P("tok", "head"), P("tok", "head"))
    return jax.shard_map(
        functools.partial(local, nz, ny, nx), mesh=mesh, in_specs=in_specs, out_specs=out_specs, check_vma=False
    )
```

```python
import functools
import math

import jax
import jax.numpy as jnp
from jax import lax
from jax.experimental import pallas as pl
from jax.experimental.pallas import tpu as pltpu
from jax.sharding import PartitionSpec as P

MESH = pl.DeviceIdType.MESH
HEAD_DIM = 128
F1, F2, F3, F4, F5, F6A, F6B, F7 = range(8)
R1, R2, R3, R4, R5, R6A, R6B, R7 = range(8, 16)
STEPS = 16
F32 = jnp.float32
BF16 = jnp.bfloat16


def dot_nt(a, b):
    return lax.dot_general(a, b, (((1,), (1,)), ((), ())), preferred_element_type=F32)


def dot_nn(a, b):
    return lax.dot_general(a, b, (((1,), (0,)), ((), ())), preferred_element_type=F32)


def dot_tn(a, b):
    return lax.dot_general(a, b, (((0,), (0,)), ((), ())), preferred_element_type=F32)


def kernel(
    heads, rows, nz, ny, nx,
    q_hbm, k_hbm, v_hbm, nb_hbm, w_hbm, g_hbm,
    packed,
    nb, q, kv, w, g, grad, grad_t, scores, probs, stats, out_t, part, send, recv, outs,
    load_sem, store_sem, send_sem, recv_sem, x_send, x_recv,
):
    position = lax.axis_index("tok")
    x = lax.axis_index("head")
    core = lax.rem(position, 2)
    y = lax.rem(position // 2, ny)
    z = position // (2 * ny)
    y_half = y // (ny // 2)
    side = 2 * core - 1
    other = 1 - core
    dz = 1 - 2 * y_half

    def tok_at(z_, y_, core_):
        return (lax.rem(z_ + nz, nz) * ny + lax.rem(y_ + ny, ny)) * 2 + core_

    partner = (tok_at(z, y, other), x)
    outer = (tok_at(z, y + side, other), x)
    far = (tok_at(z, y + ny // 2 + side, other), x)
    z_next = (tok_at(z + dz, y, core), x)
    z_prev = (tok_at(z - dz, y, core), x)
    x_right = (position, lax.rem(x + 1, nx))
    x_left = (position, lax.rem(x + nx - 1, nx))
    peers = [partner, outer, far, z_next, z_prev, x_right, x_left]

    d_model = w.shape[1]
    half = d_model // 2
    scale = 1.0 / math.sqrt(HEAD_DIM)
    scale2 = scale * math.log2(math.e)

    def load(src, dst, index):
        return pltpu.make_async_copy(src, dst, load_sem.at[index])

    def store(i, h):
        return pltpu.make_async_copy(outs.at[i, h], packed.at[i, h], store_sem.at[i, h])

    def columns(h):
        return pl.ds(h * HEAD_DIM, HEAD_DIM)

    own = pl.ds(0, rows)

    def tile(i):
        return pl.ds(i * rows, rows)

    x_rows = pl.multiple_of(x * (rows // nx), rows // nx)
    my_rows = pl.ds(x_rows, rows // nx)
    loads = {}
    for h in range(heads):
        loads["k", h] = load(k_hbm.at[:, columns(h)], kv.at[h, 0, 0, own], 3 * h)
        loads["v", h] = load(v_hbm.at[:, columns(h)], kv.at[h, 0, 1, own], 3 * h + 1)
        loads["q", h] = load(q_hbm.at[:, columns(h)], q.at[h], 3 * h + 2)
    loads["g"] = load(g_hbm, g.at[my_rows], 3 * heads)
    loads["nb"] = load(nb_hbm, nb, 3 * heads + 1)
    loads["w"] = load(w_hbm, w, 3 * heads + 2)
    for h in range(heads):
        loads["k", h].start()
        loads["v", h].start()
    loads["g"].start()
    for h in range(heads):
        loads["q", h].start()
    loads["nb"].start()
    loads["w"].start()

    barrier = pltpu.get_barrier_semaphore()
    for peer in peers:
        pl.semaphore_signal(barrier, inc=1, device_id=peer, device_id_type=MESH)
    pl.semaphore_wait(barrier, len(peers))

    def remote(h, step, src, dst, device):
        return pltpu.make_async_remote_copy(
            src_ref=src, dst_ref=dst, send_sem=send_sem.at[h, step], recv_sem=recv_sem.at[h, step],
            device_id=device, device_id_type=MESH,
        )

    def keys_of(h, group, index):
        return kv.at[h, group, :, tile(index)]

    copies = {(0, F1): remote(0, F1, kv.at[:, 0, :, tile(0)], kv.at[:, 0, :, tile(1)], partner)}
    for h in range(heads):
        copies[h, F2] = remote(h, F2, keys_of(h, 0, 0), keys_of(h, 0, 2), outer)
        copies[h, F3] = remote(h, F3, keys_of(h, 0, 0), keys_of(h, 1, 0), far)
        copies[h, F4] = remote(h, F4, keys_of(h, 1, 0), keys_of(h, 1, 1), outer)
        copies[h, F5] = remote(h, F5, keys_of(h, 1, 1), keys_of(h, 1, 2), partner)
        copies[h, F6A] = remote(h, F6A, keys_of(h, 1, 0), keys_of(h, 2, 0), z_next)
        copies[h, F6B] = remote(h, F6B, keys_of(h, 1, 1), keys_of(h, 2, 1), z_next)
        copies[h, F7] = remote(h, F7, keys_of(h, 2, 1), keys_of(h, 2, 2), partner)
        back = {R1: partner, R2: outer, R3: far, R4: outer, R5: partner, R6A: z_prev, R6B: z_prev, R7: partner}
        for step, device in back.items():
            copies[h, step] = remote(h, step, send.at[h, step - R1], recv.at[h, step - R1], device)

    def start(h, *steps):
        for step in steps:
            copies[h, step].start()

    def arrive(h, *steps):
        for step in steps:
            copies[h, step].wait_recv()

    def x_copy(index, row_block, column_block, device):
        block = g.at[pl.ds(row_block, rows // nx), pl.ds(column_block * half, half)]
        return pltpu.make_async_remote_copy(
            src_ref=block, dst_ref=block, send_sem=x_send.at[index], recv_sem=x_recv.at[index],
            device_id=device, device_id_type=MESH,
        )

    left_rows = pl.multiple_of(lax.rem(x + nx - 1, nx) * (rows // nx), rows // nx)
    right_rows = pl.multiple_of(lax.rem(x + 1, nx) * (rows // nx), rows // nx)
    x_copies = [
        x_copy(0, x_rows, 0, x_right),
        x_copy(1, x_rows, 1, x_left),
        x_copy(2, x_rows, 1, x_right),
        x_copy(3, x_rows, 0, x_left),
        x_copy(4, left_rows, 0, x_right),
        x_copy(5, right_rows, 1, x_left),
    ]

    toward = 1 - 2 * y_half
    row_offset = (0, toward, -toward)

    def entries(group):
        base = 9 + (row_offset[group] + 1) * 3 + 1
        if group == 0:
            return (base, base - side, base + side)
        return (base + side, base, base - side)

    def relay1(h):
        arrive(h, F3)
        start(h, F4, F6A, F2)

    def relay2(h):
        arrive(h, F4)
        start(h, F5, F6B)

    def relay3(h):
        arrive(h, F6B)
        start(h, F7)

    def x_relay():
        x_copies[0].wait_recv()
        x_copies[4].start()
        x_copies[1].wait_recv()
        x_copies[5].start()

    def forward(h, group):
        if group == 0:
            if h == 0:
                arrive(h, F1)
            arrive(h, F2)
        elif group == 1:
            arrive(h, F5)
        else:
            arrive(h, F6A, F7)
        query = q[h]
        top = jnp.full((1, rows), -1e30, F32)
        for i, entry in enumerate(entries(group)):
            bias = jnp.where(nb[entry, position] >= 0, 0.0, -jnp.inf).astype(F32)
            s = dot_nt(kv[h, group, 0, tile(i)], query) * scale2 + bias
            scores[tile(i)] = s
            top = jnp.maximum(top, jnp.max(s, axis=0, keepdims=True))
        total = jnp.zeros((1, rows), F32)
        attended = jnp.zeros((HEAD_DIM, rows), F32)
        for i in range(3):
            p = jnp.exp2(scores[tile(i)] - top)
            total = total + jnp.sum(p, axis=0, keepdims=True)
            p = p.astype(BF16)
            probs[h, group, tile(i)] = p
            attended = attended + dot_tn(kv[h, group, 1, tile(i)], p)
        stats[h, group, 0:1] = top
        stats[h, group, 1:2] = total
        out_t[h, group] = attended

    def project():
        loads["w"].wait()
        for index in range(2, 6):
            x_copies[index].wait_recv()
        whole = g[...]
        for h in range(heads):
            gt = dot_nt(w[pl.ds(h * HEAD_DIM, HEAD_DIM)], whole)
            grad_t[h] = gt.astype(BF16)
            grad[h] = gt.T.astype(BF16)

    def combine(h):
        tops = [stats[h, group, 0:1] for group in range(3)]
        top = jnp.maximum(jnp.maximum(tops[0], tops[1]), tops[2])
        factors = [jnp.exp2(t - top) for t in tops]
        total = sum(f * stats[h, group, 1:2] for group, f in enumerate(factors))
        attended = jnp.zeros((HEAD_DIM, rows), F32)
        for group in range(3):
            factor = factors[group] / total
            stats[h, group, 2:3] = factor
            attended = attended + out_t[h, group] * factor
        attended = attended.astype(BF16).astype(F32)
        stats[h, 0, 3:4] = jnp.sum(attended * grad_t[h].astype(F32), axis=0, keepdims=True)
        outs[0, h] = attended.T.astype(BF16)
        store(0, h).start()

    def backward(h, group, emit):
        factor = stats[h, group, 2:3]
        delta = stats[h, 0, 3:4]
        query = q[h]
        grad_rows = grad[h]
        grad_cols = grad_t[h]
        query_t = jnp.zeros((HEAD_DIM, rows), F32)
        for i in range(3):
            weights = (probs[h, group, tile(i)].astype(F32) * factor).astype(BF16)
            dprobs = dot_nn(kv[h, group, 1, tile(i)], grad_cols)
            dscores = (weights.astype(F32) * ((dprobs - delta) * scale)).astype(BF16)
            query_t = query_t + dot_tn(kv[h, group, 0, tile(i)], dscores)
            emit(i, dot_nn(dscores, query), dot_nn(weights, grad_rows))
        if group == 2:
            out_t[h, 0] = query_t
        elif group == 1:
            out_t[h, 0] += query_t
        else:
            outs[1, h] = (out_t[h, 0] + query_t).T.astype(BF16)
            store(1, h).start()

    def put(h, step, dk, dv):
        send[h, step - R1, 0] = dk.astype(BF16)
        send[h, step - R1, 1] = dv.astype(BF16)
        start(h, step)

    def keep(h, slot, dk, dv):
        part[h, slot, 0] = dk
        part[h, slot, 1] = dv

    def emit_side(h):
        def emit(i, dk, dv):
            if i == 0:
                put(h, R6A, dk, dv)
            elif i == 1:
                keep(h, 0, dk, dv)
            else:
                put(h, R7, dk, dv)
        return emit

    def emit_far(h):
        def emit(i, dk, dv):
            if i == 0:
                keep(h, 1, dk, dv)
            elif i == 1:
                keep(h, 2, dk, dv)
            else:
                put(h, R5, dk, dv)
        return emit

    def emit_own(h):
        def emit(i, dk, dv):
            if i == 0:
                keep(h, 3, dk, dv)
            elif i == 1:
                put(h, R1, dk, dv)
            else:
                put(h, R2, dk, dv)
        return emit

    def gather_sum(h, slot, step, *steps):
        arrive(h, *steps)
        for i in range(2):
            total = part[h, slot, i]
            for other_step in steps:
                total = total + recv[h, other_step - R1, i].astype(F32)
            send[h, step - R1, i] = total.astype(BF16)
        start(h, step)

    def back2(h):
        backward(h, 2, emit_side(h))

    def back1(h):
        backward(h, 1, emit_far(h))

    def back0(h):
        backward(h, 0, emit_own(h))

    def sum_side(h):
        gather_sum(h, 0, R6B, R7)

    def sum_far(h):
        gather_sum(h, 2, R4, R5, R6B)

    def sum_outer(h):
        gather_sum(h, 1, R3, R6A, R4)

    def finish(h):
        arrive(h, R1, R2, R3)
        for i in range(2):
            total = part[h, 3, i]
            for step in (R1, R2, R3):
                total = total + recv[h, step - R1, i].astype(F32)
            outs[2 + i, h] = total.astype(BF16)
            store(2 + i, h).start()

    for h in range(heads):
        loads["k", h].wait()
        loads["v", h].wait()
        start(h, F3)
    start(0, F1)
    loads["g"].wait()
    for index in range(4):
        x_copies[index].start()
    loads["nb"].wait()
    for h in range(heads):
        loads["q", h].wait()

    relay1(0)
    x_relay()
    relay2(0)
    forward(0, 1)
    relay1(1)
    forward(0, 0)
    relay3(0)
    project()
    forward(0, 2)
    relay2(1)
    combine(0)
    back2(0)
    forward(1, 1)
    sum_side(0)
    relay1(2)
    back1(0)
    relay3(1)
    forward(1, 0)
    back0(0)
    relay2(2)
    forward(1, 2)
    combine(1)
    back2(1)
    forward(2, 1)
    sum_side(1)
    relay3(2)
    back1(1)
    sum_far(0)
    forward(2, 0)
    forward(2, 2)
    combine(2)
    back2(2)
    back0(1)
    sum_side(2)
    sum_outer(0)
    back1(2)
    sum_far(1)
    back0(2)
    sum_outer(1)
    sum_far(2)
    finish(0)
    sum_outer(2)
    finish(1)
    finish(2)

    for h in range(heads):
        for step in range(STEPS):
            if (h, step) in copies:
                copies[h, step].wait_send()
        for i in range(4):
            store(i, h).wait()
    for copy in x_copies:
        copy.wait_send()


def unpack(heads, packed, *refs):
    results, scratch, in_sem, out_sem = refs[:4], refs[4], refs[5], refs[6]
    loads = []
    for i in range(4):
        for h in range(heads):
            block = scratch.at[i, :, pl.ds(h * HEAD_DIM, HEAD_DIM)]
            loads.append(pltpu.make_async_copy(packed.at[i, h], block, in_sem.at[i, h]))
    for copy in loads:
        copy.start()
    stores = [pltpu.make_async_copy(scratch.at[i], result, out_sem.at[i]) for i, result in enumerate(results)]
    for i in range(4):
        for h in range(heads):
            loads[i * heads + h].wait()
        stores[i].start()
    for copy in stores:
        copy.wait()


def local(nz, ny, nx, query_rows, key_rows, value_rows, neighbours, out_weight, out_grad):
    rows, width = query_rows.shape
    heads = width // HEAD_DIM
    d_model = out_weight.shape[1]
    hbm = pl.BlockSpec(memory_space=pltpu.HBM)
    packed = pl.pallas_call(
        functools.partial(kernel, heads, rows, nz, ny, nx),
        out_shape=jax.ShapeDtypeStruct((4, heads, rows, HEAD_DIM), BF16),
        in_specs=[hbm] * 6,
        out_specs=hbm,
        scratch_shapes=[
            pltpu.SMEM(neighbours.shape[::-1], jnp.int32),
            pltpu.VMEM((heads, rows, HEAD_DIM), BF16),
            pltpu.VMEM((heads, 3, 2, 3 * rows, HEAD_DIM), BF16),
            pltpu.VMEM((width, d_model), BF16),
            pltpu.VMEM((rows, d_model), BF16),
            pltpu.VMEM((heads, rows, HEAD_DIM), BF16),
            pltpu.VMEM((heads, HEAD_DIM, rows), BF16),
            pltpu.VMEM((3 * rows, rows), F32),
            pltpu.VMEM((heads, 3, 3 * rows, rows), BF16),
            pltpu.VMEM((heads, 3, 8, rows), F32),
            pltpu.VMEM((heads, 3, HEAD_DIM, rows), F32),
            pltpu.VMEM((heads, 4, 2, rows, HEAD_DIM), F32),
            pltpu.VMEM((heads, 8, 2, rows, HEAD_DIM), BF16),
            pltpu.VMEM((heads, 8, 2, rows, HEAD_DIM), BF16),
            pltpu.VMEM((4, heads, rows, HEAD_DIM), BF16),
            pltpu.SemaphoreType.DMA((3 * heads + 3,)),
            pltpu.SemaphoreType.DMA((4, heads)),
            pltpu.SemaphoreType.DMA((heads, STEPS)),
            pltpu.SemaphoreType.DMA((heads, STEPS)),
            pltpu.SemaphoreType.DMA((6,)),
            pltpu.SemaphoreType.DMA((6,)),
        ],
        compiler_params=pltpu.CompilerParams(
            collective_id=0, has_side_effects=True, vmem_limit_bytes=63 * 1024 * 1024
        ),
    )(query_rows, key_rows, value_rows, neighbours.T, out_weight, out_grad)
    return pl.pallas_call(
        functools.partial(unpack, heads),
        out_shape=[jax.ShapeDtypeStruct((rows, width), BF16)] * 4,
        in_specs=[hbm],
        out_specs=[hbm] * 4,
        scratch_shapes=[
            pltpu.VMEM((4, rows, width), BF16),
            pltpu.SemaphoreType.DMA((4, heads)),
            pltpu.SemaphoreType.DMA((4,)),
        ],
    )(packed)


def solution(mesh):
    nx = mesh.shape["head"]
    ny = 8
    nz = mesh.shape["tok"] // (2 * ny)
    in_specs = (
        P("tok", "head"),
        P("tok", "head"),
        P("tok", "head"),
        P(),
        P("head", None),
        P(("tok", "head"), None),
    )
    out_specs = (P("tok", "head"), P("tok", "head"), P("tok", "head"), P("tok", "head"))
    return jax.shard_map(
        functools.partial(local, nz, ny, nx), mesh=mesh, in_specs=in_specs, out_specs=out_specs, check_vma=False
    )
```
